32 devices in a mesh: groups: 2 (over x), orient: 8 (over z, y), img: 2 (over core).
Axes of the slice: x: 2, y: 2, z: 4, core: 2. Of those that a mesh axis runs over, the one named last changes fastest.
Arguments:
- images: bfloat16 [256, 16384], P(('groups', 'orient', 'img')), parts along dimension 0, may hold values from -600 to 600
- image_shift: int32 [256, 2], P(('groups', 'orient', 'img')), parts along dimension 0, may hold values from -4 to 4
- image_group: int32 [256], P(('groups', 'orient', 'img')), parts along dimension 0, may hold values from 0 to 7
- projections: bfloat16 [2816, 16384], P(('orient', 'img')), may hold values from -0.48 to 0.48
- slice_class: int32 [2816], P(('orient', 'img')), may hold values from 0 to 23
- slice_angle: int32 [2816], P(('orient', 'img')), may hold values from 0 to 4607
- log_prior: float32 [24, 4608], replicated, may hold values from -3 to 0
- ctf_table: float32 [8, 8192], replicated, may hold values from -1 to 1
Outputs:
- weighted_sums: bfloat16 [5632, 16384], P(('groups', 'orient', 'img')), parts along dimension 0
- group_mass: float32 [8, 5632], P(None, ('groups', 'orient', 'img')), parts along dimension 1
- class_posterior: float32 [256, 24], P(('groups', 'orient', 'img')), parts along dimension 0
- log_evidence: float32 [256], P(('groups', 'orient', 'img')), parts along dimension 0
The draws below stay inside these ranges and needn't reach their ends.
There are 2 independent parts, one for each index of `groups`. The reference program is written for one: setup_inputs(seed, part) draws one part's arguments, and reference() takes and returns one part's arrays. A program takes and returns all parts, laid end to end along the dimension named above; an argument that names none is the same for every part. Nothing has to cross between parts.
All inputs are finite; a program needn't handle non-finite values.
Results may differ from the reference program's by a relative error of at most 0.0045.
Values may be sent and summed in bfloat16 or wider, within the bound.
A program may use at most 128 MiB of HBM per device.

```python
import math
import jax
import jax.numpy as jnp
from jax import lax

KY = 128
KX = 64
HALF = 8192
FEAT = 16384
CLASSES = 24
ORIENTS = 4608
GROUPS = 8
BOX = 128
PROJ_DEV = 176
IMG = 128
PROJ = 2816
N_ORIENT = 8
N_IMG = 2


def draw_projections(key, part):
    key = jax.random.fold_in(key, 11)
    key_scale, key_values = jax.random.split(key)
    scales = jnp.exp(jax.random.uniform(key_scale, (PROJ, 1), jnp.float32, math.log(0.008), math.log(0.08)))
    values = jnp.clip(jax.random.normal(key_values, (PROJ, FEAT), jnp.float32), -6.0, 6.0)
    return (values * scales).astype(jnp.bfloat16)


def draw_images(key, part):
    key = jax.random.fold_in(key, 23)
    key_noise = jax.random.fold_in(key, 0)
    noise_field = jnp.clip(jax.random.normal(key_noise, (IMG, FEAT), jnp.float32), -6.0, 6.0)
    row_index = jnp.arange(IMG, dtype=jnp.int32)
    spread = jnp.ones((IMG,), jnp.float32)
    strong = 1500.0 / math.sqrt(FEAT) * jnp.exp2((row_index // 37 % 3).astype(jnp.float32))
    factors = jnp.where(row_index % 37 == 5, strong, spread)
    noise_field = jnp.clip(noise_field * factors[:, None], -600.0, 600.0)
    return noise_field.astype(jnp.bfloat16)


def touch_ends(values, key, low, top_value):
    dims = values.shape
    index_at = [jax.random.randint(jax.random.fold_in(key, axis), (), 0, dims[axis]) for axis in range(len(dims))]
    values = values.at[tuple(index_at)].set(low)
    longest = dims.index(max(dims))
    index_at[longest] = (index_at[longest] + 1) % dims[longest]
    return values.at[tuple(index_at)].set(top_value)


def setup_inputs(seed: int = 0, part: int = 0) -> dict:
    key_of = jax.random.split(jax.random.key(seed), 9)
    part_keys = jax.random.split(jax.random.fold_in(key_of[8], part), 9)
    images = draw_images(jax.random.fold_in(jax.random.fold_in(key_of[8], part), 71), part)
    image_shift = touch_ends(jax.random.randint(part_keys[1], (IMG, 2), -4, 5), jax.random.fold_in(part_keys[1], 1), -4, 4).astype(jnp.int32)
    image_group = touch_ends(jax.random.randint(part_keys[2], (IMG,), 0, GROUPS), jax.random.fold_in(part_keys[2], 1), 0, GROUPS - 1).astype(jnp.int32)
    projections = draw_projections(jax.random.fold_in(key_of[8], 71), part)
    slice_class = touch_ends(jax.random.randint(key_of[4], (PROJ,), 0, CLASSES), jax.random.fold_in(key_of[4], 1), 0, CLASSES - 1).astype(jnp.int32)
    slice_angle = touch_ends(jax.random.randint(key_of[5], (PROJ,), 0, ORIENTS), jax.random.fold_in(key_of[5], 1), 0, ORIENTS - 1).astype(jnp.int32)
    log_prior = jnp.clip(jax.random.uniform(key_of[6], (CLASSES, ORIENTS), jnp.float32, -3.0, 0.0), -3.0, 0.0)
    ctf_table = jnp.clip(jax.random.uniform(key_of[7], (GROUPS, HALF), jnp.float32, -1.0, 1.0), -1.0, 1.0)
    return {"images": images, "image_shift": image_shift, "image_group": image_group, "projections": projections, "slice_class": slice_class, "slice_angle": slice_angle, "log_prior": log_prior, "ctf_table": ctf_table}


def prepare_rows(images, image_shift, contrast):
    row_count = images.shape[0]
    real_part = images[:, :HALF].astype(jnp.float32)
    imag_part = images[:, HALF:].astype(jnp.float32)
    freq_y = (jnp.arange(KY, dtype=jnp.int32) - KY // 2).astype(jnp.float32)
    freq_x = jnp.arange(KX, dtype=jnp.int32).astype(jnp.float32)
    shift_x = image_shift[:, 0].astype(jnp.float32)
    shift_y = image_shift[:, 1].astype(jnp.float32)
    phases = (2.0 * math.pi / BOX) * (shift_y[:, None, None] * freq_y[None, :, None] + shift_x[:, None, None] * freq_x[None, None, :])
    phases = phases.reshape(row_count, HALF)
    cosine = jnp.cos(phases)
    sine_part = jnp.sin(phases)
    moved_real = contrast * (real_part * cosine + imag_part * sine_part)
    moved_imag = contrast * (imag_part * cosine - real_part * sine_part)
    return jnp.concatenate([moved_real, moved_imag], axis=1).astype(jnp.bfloat16)


def reference(images, image_shift, image_group, projections, slice_class, slice_angle, log_prior, ctf_table):
    prepared = prepare_rows(images, image_shift, ctf_table[image_group])
    group_hot = (image_group[:, None] == jnp.arange(GROUPS, dtype=jnp.int32)[None, :]).astype(jnp.float32)
    squared_ctf = ctf_table * ctf_table
    blocks = N_ORIENT * N_IMG
    proj_blocks = projections.reshape(blocks, PROJ_DEV, FEAT)
    prior_rows = jnp.take(log_prior.reshape(-1), slice_class * ORIENTS + slice_angle).reshape(blocks, PROJ_DEV)

    def block_scores(operands):
        block, prior_block = operands
        raw = lax.dot_general(prepared, block, (((1,), (1,)), ((), ())), preferred_element_type=jnp.float32)
        real_block = block[:, :HALF].astype(jnp.float32)
        imag_block = block[:, HALF:].astype(jnp.float32)
        powers = real_block * real_block + imag_block * imag_block
        per_group = jnp.dot(squared_ctf, powers.T, precision=lax.Precision.HIGHEST)
        return raw - 0.5 * per_group[image_group] + prior_block[None, :]

    scores = lax.map(block_scores, (proj_blocks, prior_rows))
    scores = jnp.transpose(scores, (1, 0, 2)).reshape(IMG, PROJ)
    maxima = jnp.max(scores, axis=1)
    exponent = jnp.exp(scores - maxima[:, None])
    totals = jnp.sum(exponent, axis=1)
    class_hot = (slice_class[:, None] == jnp.arange(CLASSES, dtype=jnp.int32)[None, :]).astype(jnp.float32)
    class_mass = jnp.dot(exponent, class_hot, precision=lax.Precision.HIGHEST)
    weights = (exponent / totals[:, None]).astype(jnp.bfloat16)
    weight_blocks = jnp.transpose(weights.reshape(IMG, blocks, PROJ_DEV), (1, 0, 2))

    def block_sums(block):
        return lax.dot_general(block, prepared, (((0,), (0,)), ((), ())), preferred_element_type=jnp.float32).astype(jnp.bfloat16)

    weighted_sums = lax.map(block_sums, weight_blocks).reshape(PROJ, FEAT)
    group_mass = lax.dot_general(group_hot.astype(jnp.bfloat16), weights, (((0,), (0,)), ((), ())), preferred_element_type=jnp.float32)
    class_posterior = class_mass / totals[:, None]
    log_evidence = maxima + jnp.log(totals)
    return (weighted_sums, group_mass, class_posterior, log_evidence)
```

```python
import functools
import math

import jax
import jax.numpy as jnp
from jax import lax
from jax.experimental import pallas as pl
from jax.experimental.pallas import tpu as pltpu
from jax.sharding import PartitionSpec as P

KY = 128
KX = 64
HALF = 8192
BOX = 128
LANES = 128
PIECES = 2
CHUNK = 1024
TILE = 1024
STEP = 2.0 * math.pi / BOX
MESH = pl.DeviceIdType.MESH
NT = (((1,), (1,)), ((), ()))
TN = (((0,), (0,)), ((), ()))


def split3(x):
    hi = x.astype(jnp.bfloat16)
    rest = x - hi.astype(jnp.float32)
    mid = rest.astype(jnp.bfloat16)
    low = (rest - mid.astype(jnp.float32)).astype(jnp.bfloat16)
    return hi, mid, low


def dot32(a, b, dims):
    return lax.dot_general(a, b, dims, preferred_element_type=jnp.float32)


def gather_kernel(
    n_orient,
    n_img,
    rows,
    images,
    shift,
    group,
    proj_hbm,
    slice_class,
    slice_angle,
    prior_hbm,
    ctf,
    g_out,
    w_out,
    mass_out,
    cls_out,
    lev_out,
    proj,
    prior,
    gat,
    scores,
    per_group,
    stat_src,
    stat_dst,
    own_src,
    own_dst,
    load_sem,
    ring_send,
    ring_recv,
    sib_send,
    sib_recv,
    out_sem,
    stat_send,
    stat_recv,
    own_send,
    own_recv,
):
    n_dev = n_orient * n_img
    n_all = n_dev * rows
    n_proj = proj.shape[0]
    n_cls, n_ang = prior.shape
    half_ring = n_orient // 2
    orient = lax.axis_index("orient")
    core = lax.axis_index("img")
    me = orient * n_img + core

    if n_orient == 8:
        spot = orient // 2 + (orient % 2) * (7 - 2 * (orient // 2))

        def orient_at(q):
            return 2 * (q % 4 + (q // 4) * (3 - 2 * (q % 4))) + q // 4

    else:
        spot = orient

        def orient_at(q):
            return q

    def chip(delta):
        return orient_at((spot + delta + n_orient) % n_orient)

    barrier = pltpu.get_barrier_semaphore()
    for r in range(1, n_dev):
        other = (me + r) % n_dev
        pl.semaphore_signal(
            barrier,
            inc=1,
            device_id={"orient": other // n_img, "img": other % n_img},
            device_id_type=MESH,
        )
    load_proj = pltpu.make_async_copy(proj_hbm, proj, load_sem.at[0])
    load_prior = pltpu.make_async_copy(prior_hbm, prior, load_sem.at[1])
    load_proj.start()
    load_prior.start()

    tx = shift[:, 0:1]
    ty = shift[:, 1:2]
    lane = lax.broadcasted_iota(jnp.int32, (rows, CHUNK), 1)
    inner = (tx * (lane % KX) + ty * (lane // KX)) & (BOX - 1)
    inner = inner.astype(jnp.float32) * STEP
    cos_in, sin_in = jnp.cos(inner), jnp.sin(inner)
    groups = group[...]
    reps = CHUNK // LANES

    def prepare(j, carry):
        start = pl.multiple_of(j * CHUNK, CHUNK)
        outer = (ty * (j * (CHUNK // KX) - KY // 2)) & (BOX - 1)
        outer = jnp.broadcast_to(outer, (rows, LANES)).astype(jnp.float32) * STEP
        cos_o = jnp.concatenate([jnp.cos(outer)] * reps, axis=1)
        sin_o = jnp.concatenate([jnp.sin(outer)] * reps, axis=1)
        cosine = cos_o * cos_in - sin_o * sin_in
        sine = sin_o * cos_in + cos_o * sin_in
        g = jnp.zeros((rows, CHUNK), jnp.float32)
        for h in range(ctf.shape[0]):
            g = jnp.where(groups == h, ctf[h : h + 1, pl.ds(start, CHUNK)], g)
        a = images[:, pl.ds(start, CHUNK)].astype(jnp.float32)
        b = images[:, pl.ds(pl.multiple_of(HALF + start, CHUNK), CHUNK)].astype(jnp.float32)
        moved = jnp.concatenate([g * (a * cosine + b * sine), g * (b * cosine - a * sine)], axis=0)
        gat[me, :, pl.ds(start, CHUNK)] = moved.astype(jnp.bfloat16)
        return carry

    lax.fori_loop(0, HALF // CHUNK, prepare, 0)
    tag = jnp.broadcast_to(groups.astype(jnp.float32), (rows, LANES))
    gat[me, :, HALF : HALF + LANES] = jnp.concatenate([tag, tag], axis=0).astype(jnp.bfloat16)

    width = HALF // PIECES
    length = (half_ring - 1) * PIECES + PIECES // 2

    def piece_of(direction, k):
        return (k % PIECES + direction * (PIECES // 2)) % PIECES

    def columns(p):
        return pl.ds(p * width, width + (LANES if p == PIECES - 1 else 0))

    def ring_copy(direction, k):
        step = k // PIECES
        source = chip(-step if direction == 0 else step) * n_img + core
        block = gat.at[source, :, columns(piece_of(direction, k))]
        return pltpu.make_async_remote_copy(
            src_ref=block,
            dst_ref=block,
            send_sem=ring_send.at[direction, k],
            recv_sem=ring_recv.at[direction, k],
            device_id={"orient": chip(1 if direction == 0 else -1), "img": core},
            device_id_type=MESH,
        )

    def ring_arrival(direction, k):
        step = 1 + k // PIECES
        source = chip(-step if direction == 0 else step) * n_img + core
        block = gat.at[source, :, columns(piece_of(direction, k))]
        return pltpu.make_async_remote_copy(
            src_ref=block,
            dst_ref=block,
            send_sem=ring_send.at[direction, k],
            recv_sem=ring_recv.at[direction, k],
            device_id={"orient": chip(1 if direction == 0 else -1), "img": core},
            device_id_type=MESH,
        )

    def sib_copy(index, delta, p, side):
        source = chip(delta) * n_img + (core if side == 0 else 1 - core)
        block = gat.at[source, :, columns(p)]
        return pltpu.make_async_remote_copy(
            src_ref=block,
            dst_ref=block,
            send_sem=sib_send.at[index],
            recv_sem=sib_recv.at[index],
            device_id={"orient": orient, "img": 1 - core},
            device_id_type=MESH,
        )

    def sib_args(direction, k):
        step = 1 + k // PIECES
        return (
            PIECES + 2 * k + direction,
            -step if direction == 0 else step,
            piece_of(direction, k),
        )

    pl.semaphore_wait(barrier, n_dev - 1)
    for k in range(PIECES):
        for direction in range(2):
            ring_copy(direction, k).start()
    for p in range(PIECES):
        sib_copy(p, 0, p, 0).start()

    def power_chunks(first, last):
        def step(j, acc):
            start = pl.multiple_of(j * 512, 512)
            re = proj[:, pl.ds(start, 512)].astype(jnp.float32)
            im = proj[:, pl.ds(pl.multiple_of(HALF + start, 512), 512)].astype(jnp.float32)
            parts = split3(re * re + im * im)
            table = ctf[:, pl.ds(start, 512)]
            t_hi, t_mid, t_low = split3(table * table)
            pair = jnp.concatenate(
                [t_hi.astype(jnp.float32), t_mid.astype(jnp.float32), t_low.astype(jnp.float32)], 0
            ).astype(jnp.bfloat16)
            for part in parts:
                acc = acc + dot32(pair, part, NT)
            return acc

        acc = jnp.zeros((3 * ctf.shape[0], n_proj), jnp.float32)
        acc = lax.fori_loop(first, last, step, acc)
        n = ctf.shape[0]
        total = acc[:n] + acc[n : 2 * n] + acc[2 * n :]
        per_group[...] = total if first == 0 else per_group[...] + total

    classes = slice_class[...]
    angles = slice_angle[...]

    def prior_row():
        hot = (lax.broadcasted_iota(jnp.int32, (n_ang, n_proj), 0) == angles).astype(jnp.float32)
        hot = hot.astype(jnp.bfloat16)
        total = jnp.zeros((n_cls, n_proj), jnp.float32)
        for part in split3(prior[...]):
            total = total + lax.dot_general(
                part, hot, (((1,), (0,)), ((), ())), preferred_element_type=jnp.float32
            )
        own = lax.broadcasted_iota(jnp.int32, (n_cls, n_proj), 0) == classes
        return jnp.sum(jnp.where(own, total, 0.0), axis=0, keepdims=True)

    def score(blocks, first, last, fresh):
        def step(j, carry):
            start = pl.multiple_of(j * 512, 512)
            left = jnp.concatenate([gat[d, :, pl.ds(start, 512)] for d in blocks], axis=0)
            re = proj[:, pl.ds(start, 512)]
            im = proj[:, pl.ds(pl.multiple_of(HALF + start, 512), 512)]
            return carry[0] + dot32(left, re, NT), carry[1] + dot32(left, im, NT)

        zero = jnp.zeros((len(blocks) * 2 * rows, n_proj), jnp.float32)
        a, b = lax.fori_loop(first, last, step, (zero, zero))
        for i, d in enumerate(blocks):
            base = 2 * rows * i
            part = a[base : base + rows] + b[base + rows : base + 2 * rows]
            scores[d] = part if fresh else scores[d] + part

    def both(delta):
        return [chip(delta) * n_img, chip(delta) * n_img + 1]

    out_copies = []

    def put_out(blocks):
        for d in blocks:
            copy = pltpu.make_async_copy(gat.at[d], g_out.at[d], out_sem.at[len(out_copies)])
            copy.start()
            out_copies.append(copy)

    n_power = HALF // 512
    for k in range(length):
        for direction in range(2):
            ring_arrival(direction, k).wait_recv()
            ahead = k + PIECES
            if ahead < length:
                ring_copy(direction, ahead).start()
            index, delta, p = sib_args(direction, k)
            sib_copy(index, delta, p, 0).start()
        if k == 0:
            load_proj.wait()
            load_prior.wait()
            prior_here = prior_row()
            power_chunks(0, n_power // 2)
        if k == 1:
            power_chunks(n_power // 2, n_power)
        if k == 2:
            for q in range(PIECES):
                sib_copy(q, 0, q, 1).wait_recv()
            score(both(0), 0, HALF // 512, True)
            put_out(both(0))
        if k >= PIECES and k % PIECES == min(1, PIECES - 1):
            step = k // PIECES
            for q in range((step - 1) * PIECES, step * PIECES):
                for direction in range(2):
                    index, delta, p = sib_args(direction, q)
                    sib_copy(index, delta, p, 1).wait_recv()
            blocks = both(-step) + both(step)
            score(blocks, 0, HALF // 512, True)
            put_out(blocks)

    step = half_ring - 1
    if (half_ring - 1) * PIECES + min(1, PIECES - 1) >= length:
        for q in range((step - 1) * PIECES, step * PIECES):
            for direction in range(2):
                index, delta, p = sib_args(direction, q)
                sib_copy(index, delta, p, 1).wait_recv()
        blocks = both(-step) + both(step)
        score(blocks, 0, HALF // 512, True)
        put_out(blocks)
    blocks = both(half_ring)
    for k in range((half_ring - 1) * PIECES, length):
        for direction in range(2):
            index, delta, p = sib_args(direction, k)
            sib_copy(index, delta, p, 1).wait_recv()
    score(blocks, 0, HALF // 512, True)
    put_out(blocks)

    tags = gat[:, :, HALF : HALF + LANES].astype(jnp.float32)
    tags = tags[:, :rows, :].reshape(n_all, LANES)
    tag_col = tags[:, 0:1]
    full = scores[...].reshape(n_all, n_proj)
    energy = jnp.zeros((n_all, n_proj), jnp.float32)
    for h in range(ctf.shape[0]):
        energy = jnp.where(tag_col == h, per_group[h : h + 1, :], energy)
    full = full - 0.5 * energy + prior_here
    top = jnp.max(full, axis=1, keepdims=True)
    expo = jnp.exp(full - top)
    slot = lax.broadcasted_iota(jnp.int32, (LANES, n_proj), 0)
    hot = jnp.where(slot == n_cls, 1.0, jnp.where(slot == classes, 1.0, 0.0)).astype(jnp.bfloat16)
    mass = jnp.zeros((n_all, LANES), jnp.float32)
    for part in split3(expo):
        mass = mass + dot32(part, hot, NT)
    mass = jnp.where(lax.broadcasted_iota(jnp.int32, (n_all, LANES), 1) == n_cls + 1, top, mass)
    turned = mass.T
    stat_src[...] = turned[n_cls : n_cls + 2, :]
    own_src[...] = mass.reshape(n_dev, rows, LANES)

    def stat_copy(r):
        other = (me + r) % n_dev
        return pltpu.make_async_remote_copy(
            src_ref=stat_src,
            dst_ref=stat_dst.at[me],
            send_sem=stat_send.at[r],
            recv_sem=stat_recv.at[r],
            device_id={"orient": other // n_img, "img": other % n_img},
            device_id_type=MESH,
        )

    def own_copy(r):
        other = (me + r) % n_dev
        return pltpu.make_async_remote_copy(
            src_ref=own_src.at[other],
            dst_ref=own_dst.at[me],
            send_sem=own_send.at[r],
            recv_sem=own_recv.at[r],
            device_id={"orient": other // n_img, "img": other % n_img},
            device_id_type=MESH,
        )

    def stat_arrival(r):
        source = (me - r + n_dev) % n_dev
        return pltpu.make_async_remote_copy(
            src_ref=stat_src,
            dst_ref=stat_dst.at[source],
            send_sem=stat_send.at[r],
            recv_sem=stat_recv.at[r],
            device_id={"orient": source // n_img, "img": source % n_img},
            device_id_type=MESH,
        )

    def own_arrival(r):
        source = (me - r + n_dev) % n_dev
        return pltpu.make_async_remote_copy(
            src_ref=own_src.at[source],
            dst_ref=own_dst.at[source],
            send_sem=own_send.at[r],
            recv_sem=own_recv.at[r],
            device_id={"orient": source // n_img, "img": source % n_img},
            device_id_type=MESH,
        )

    for r in range(1, n_dev):
        stat_copy(r).start()
    for r in range(1, n_dev):
        own_copy(r).start()
    stat_dst[me] = stat_src[...]
    own_dst[me] = own_src[me]
    for r in range(1, n_dev):
        stat_arrival(r).wait_recv()
    best = stat_dst[0, 1:2, :]
    for d in range(1, n_dev):
        best = jnp.maximum(best, stat_dst[d, 1:2, :])
    total = jnp.zeros_like(best)
    for d in range(n_dev):
        total = total + jnp.exp(stat_dst[d, 1:2, :] - best) * stat_dst[d, 0:1, :]
    factor = jnp.exp(stat_src[1:2, :] - best) / total
    factor = jnp.broadcast_to(factor, (LANES, n_all)).T[:, 0:1]
    weights = (expo * factor).astype(jnp.bfloat16)
    spread_r = lax.broadcasted_iota(jnp.int32, (n_all, 2 * n_all), 0)
    spread_c = lax.broadcasted_iota(jnp.int32, (n_all, 2 * n_all), 1)
    place = 2 * rows * (spread_r // rows) + spread_r % rows
    for part in range(2):
        spread = jnp.where(spread_c == place + part * rows, 1.0, 0.0).astype(jnp.bfloat16)
        w_out[part] = dot32(weights, spread, TN).astype(jnp.bfloat16)
    lanes = lax.broadcasted_iota(jnp.int32, (n_all, LANES), 1).astype(jnp.float32)
    member = jnp.where(tags == lanes, 1.0, 0.0).astype(jnp.bfloat16)
    mass_out[...] = dot32(member, weights, TN)[: ctf.shape[0]]

    for r in range(1, n_dev):
        own_arrival(r).wait_recv()
    best = own_dst[0, :, n_cls + 1 : n_cls + 2]
    for d in range(1, n_dev):
        best = jnp.maximum(best, own_dst[d, :, n_cls + 1 : n_cls + 2])
    sums = jnp.zeros((rows, LANES), jnp.float32)
    for d in range(n_dev):
        sums = sums + jnp.exp(own_dst[d, :, n_cls + 1 : n_cls + 2] - best) * own_dst[d]
    total = sums[:, n_cls : n_cls + 1]
    cls_out[...] = sums[:, :n_cls] / total
    lev_out[...] = best + jnp.log(total)

    for direction in range(2):
        for k in range(length):
            ring_copy(direction, k).wait_send()
            index, delta, p = sib_args(direction, k)
            sib_copy(index, delta, p, 0).wait_send()
    for p in range(PIECES):
        sib_copy(p, 0, p, 0).wait_send()
    for r in range(1, n_dev):
        stat_copy(r).wait_send()
        own_copy(r).wait_send()
    for copy in out_copies:
        copy.wait()


def sum_kernel(g_ref, w_ref, mass_ref, cls_ref, lev_ref, out_ref, mass_out, cls_out, lev_out):
    part = pl.program_id(1)

    @pl.when((pl.program_id(0) == 0) & (part == 0))
    def _():
        mass_out[...] = mass_ref[...]
        cls_out[...] = cls_ref[...]
        lev_out[...] = lev_ref[...]

    g = g_ref[...].reshape(w_ref.shape[2], out_ref.shape[1])
    out_ref[...] = jnp.dot(w_ref[part], g, preferred_element_type=jnp.float32).astype(jnp.bfloat16)


def body(
    n_orient,
    n_img,
    images,
    image_shift,
    image_group,
    projections,
    slice_class,
    slice_angle,
    log_prior,
    ctf_table,
):
    n_dev = n_orient * n_img
    rows = images.shape[0]
    n_all = n_dev * rows
    n_proj, feat = projections.shape
    n_grp = ctf_table.shape[0]
    n_cls = log_prior.shape[0]
    length = (n_orient // 2 - 1) * PIECES + PIECES // 2
    vmem = pl.BlockSpec(memory_space=pltpu.VMEM)
    hbm = pl.BlockSpec(memory_space=pl.ANY)
    f32, bf16 = jnp.float32, jnp.bfloat16
    dma = pltpu.SemaphoreType.DMA
    g, w, mass, cls, lev = pl.pallas_call(
        functools.partial(gather_kernel, n_orient, n_img, rows),
        out_shape=(
            jax.ShapeDtypeStruct((n_dev, 2 * rows, HALF + LANES), bf16),
            jax.ShapeDtypeStruct((2, n_proj, 2 * n_all), bf16),
            jax.ShapeDtypeStruct((n_grp, n_proj), f32),
            jax.ShapeDtypeStruct((rows, n_cls), f32),
            jax.ShapeDtypeStruct((rows, 1), f32),
        ),
        in_specs=[vmem, vmem, vmem, hbm, vmem, vmem, hbm, vmem],
        out_specs=(hbm, vmem, vmem, vmem, vmem),
        scratch_shapes=[
            pltpu.VMEM((n_proj, feat), bf16),
            pltpu.VMEM(log_prior.shape, f32),
            pltpu.VMEM((n_dev, 2 * rows, HALF + LANES), bf16),
            pltpu.VMEM((n_dev, rows, n_proj), f32),
            pltpu.VMEM((n_grp, n_proj), f32),
            pltpu.VMEM((2, n_all), f32),
            pltpu.VMEM((n_dev, 2, n_all), f32),
            pltpu.VMEM((n_dev, rows, LANES), f32),
            pltpu.VMEM((n_dev, rows, LANES), f32),
            dma((2,)),
            dma((2, length)),
            dma((2, length)),
            dma((2 * length + PIECES,)),
            dma((2 * length + PIECES,)),
            dma((n_dev,)),
            dma((n_dev,)),
            dma((n_dev,)),
            dma((n_dev,)),
            dma((n_dev,)),
        ],
        compiler_params=pltpu.CompilerParams(
            collective_id=0, has_side_effects=True, vmem_limit_bytes=48 * 2**20
        ),
    )(
        images,
        image_shift,
        image_group.reshape(rows, 1),
        projections,
        slice_class.reshape(1, n_proj),
        slice_angle.reshape(1, n_proj),
        log_prior,
        ctf_table,
    )
    tiles = HALF // TILE
    once = lambda shape: pl.BlockSpec(shape, lambda j, part: (0,) * len(shape))
    out, mass, cls, lev = pl.pallas_call(
        sum_kernel,
        grid=(tiles, 2),
        out_shape=(
            jax.ShapeDtypeStruct((n_proj, feat), bf16),
            jax.ShapeDtypeStruct(mass.shape, f32),
            jax.ShapeDtypeStruct(cls.shape, f32),
            jax.ShapeDtypeStruct(lev.shape, f32),
        ),
        in_specs=[
            pl.BlockSpec((n_dev, 2 * rows, TILE), lambda j, part: (0, 0, j)),
            once(w.shape),
            once(mass.shape),
            once(cls.shape),
            once(lev.shape),
        ],
        out_specs=(
            pl.BlockSpec((n_proj, TILE), lambda j, part: (0, part * tiles + j)),
            once(mass.shape),
            once(cls.shape),
            once(lev.shape),
        ),
        compiler_params=pltpu.CompilerParams(vmem_limit_bytes=48 * 2**20),
    )(g, w, mass, cls, lev)
    return out, mass, cls, lev.reshape(rows)


def solution(mesh):
    in_specs = (
        P(("groups", "orient", "img"), None),
        P(("groups", "orient", "img"), None),
        P(("groups", "orient", "img")),
        P(("orient", "img"), None),
        P(("orient", "img")),
        P(("orient", "img")),
        P(),
        P(),
    )
    out_specs = (
        P(("groups", "orient", "img"), None),
        P(None, ("groups", "orient", "img")),
        P(("groups", "orient", "img"), None),
        P(("groups", "orient", "img")),
    )
    return jax.shard_map(
        functools.partial(body, mesh.shape["orient"], mesh.shape["img"]),
        mesh=mesh,
        in_specs=in_specs,
        out_specs=out_specs,
        check_vma=False,
    )
```

```python
import functools
import math

import jax
import jax.numpy as jnp
from jax import lax
from jax.experimental import pallas as pl
from jax.experimental.pallas import tpu as pltpu
from jax.sharding import PartitionSpec as P

KY = 128
KX = 64
HALF = 8192
BOX = 128
LANES = 128
PIECES = 4
CHUNK = 1024
TILE = 2048
VMEM_BYTES = 64 * 2**20
STEP = 2.0 * math.pi / BOX
MESH = pl.DeviceIdType.MESH
NT = (((1,), (1,)), ((), ()))
TN = (((0,), (0,)), ((), ()))


def split3(x):
    hi = x.astype(jnp.bfloat16)
    rest = x - hi.astype(jnp.float32)
    mid = rest.astype(jnp.bfloat16)
    low = (rest - mid.astype(jnp.float32)).astype(jnp.bfloat16)
    return hi, mid, low


def dot32(a, b, dims):
    return lax.dot_general(a, b, dims, preferred_element_type=jnp.float32)


def gather_kernel(
    n_orient,
    n_img,
    rows,
    images_hbm,
    shift_hbm,
    group_hbm,
    proj_hbm,
    class_hbm,
    angle_hbm,
    prior_hbm,
    ctf_hbm,
    g_out,
    w_out,
    mass_out,
    cls_out,
    lev_out,
    images,
    shift_row,
    group_row,
    proj,
    slice_class,
    slice_angle,
    prior,
    ctf,
    gat,
    scores,
    per_group,
    stat_src,
    stat_dst,
    own_src,
    own_dst,
    load_sem,
    ring_send,
    ring_recv,
    sib_send,
    sib_recv,
    out_sem,
    stat_send,
    stat_recv,
    own_send,
    own_recv,
):
    n_dev = n_orient * n_img
    n_all = n_dev * rows
    n_proj = proj.shape[0]
    n_cls, n_ang = prior.shape
    half_ring = n_orient // 2
    orient = lax.axis_index("orient")
    core = lax.axis_index("img")
    me = orient * n_img + core

    if n_orient == 8:
        spot = orient // 2 + (orient % 2) * (7 - 2 * (orient // 2))

        def orient_at(q):
            return 2 * (q % 4 + (q // 4) * (3 - 2 * (q % 4))) + q // 4

    else:
        spot = orient

        def orient_at(q):
            return q

    def chip(delta):
        return orient_at((spot + delta + n_orient) % n_orient)

    barrier = pltpu.get_barrier_semaphore()
    for r in range(1, n_dev):
        other = (me + r) % n_dev
        pl.semaphore_signal(
            barrier,
            inc=1,
            device_id={"orient": other // n_img, "img": other % n_img},
            device_id_type=MESH,
        )
    loads = [
        pltpu.make_async_copy(source, place, load_sem.at[i])
        for i, (source, place) in enumerate(
            (
                (shift_hbm, shift_row),
                (group_hbm, group_row),
                (ctf_hbm, ctf),
                (images_hbm, images),
                (class_hbm, slice_class),
                (angle_hbm, slice_angle),
                (prior_hbm, prior),
                (proj_hbm, proj),
            )
        )
    ]
    for load in loads:
        load.start()
    diagonal = lax.broadcasted_iota(jnp.int32, (rows, rows), 0) == lax.broadcasted_iota(
        jnp.int32, (rows, rows), 1
    )

    def column(row):
        return jnp.sum(jnp.where(diagonal, row, 0.0), axis=1, keepdims=True)

    for load in loads[:4]:
        load.wait()

    tx = column(shift_row[0:1, :].astype(jnp.float32)).astype(jnp.int32)
    ty = column(shift_row[1:2, :].astype(jnp.float32)).astype(jnp.int32)
    lane = lax.broadcasted_iota(jnp.int32, (rows, CHUNK), 1)
    inner = (tx * (lane % KX) + ty * (lane // KX)) & (BOX - 1)
    inner = inner.astype(jnp.float32) * STEP
    cos_in, sin_in = jnp.cos(inner), jnp.sin(inner)
    groups = column(group_row[...].astype(jnp.float32)).astype(jnp.int32)
    reps = CHUNK // LANES

    def prepare(j, carry):
        start = pl.multiple_of(j * CHUNK, CHUNK)
        outer = (ty * (j * (CHUNK // KX) - KY // 2)) & (BOX - 1)
        outer = jnp.broadcast_to(outer, (rows, LANES)).astype(jnp.float32) * STEP
        cos_o = jnp.concatenate([jnp.cos(outer)] * reps, axis=1)
        sin_o = jnp.concatenate([jnp.sin(outer)] * reps, axis=1)
        cosine = cos_o * cos_in - sin_o * sin_in
        sine = sin_o * cos_in + cos_o * sin_in
        g = jnp.zeros((rows, CHUNK), jnp.float32)
        for h in range(ctf.shape[0]):
            g = jnp.where(groups == h, ctf[h : h + 1, pl.ds(start, CHUNK)], g)
        a = images[:, pl.ds(start, CHUNK)].astype(jnp.float32)
        b = images[:, pl.ds(pl.multiple_of(HALF + start, CHUNK), CHUNK)].astype(jnp.float32)
        moved = jnp.concatenate([g * (a * cosine + b * sine), g * (b * cosine - a * sine)], axis=0)
        gat[me, :, pl.ds(start, CHUNK)] = moved.astype(jnp.bfloat16)
        return carry

    lax.fori_loop(0, HALF // CHUNK, prepare, 0)
    tag = jnp.broadcast_to(groups.astype(jnp.float32), (rows, LANES))
    gat[me, :, HALF : HALF + LANES] = jnp.concatenate([tag, tag], axis=0).astype(jnp.bfloat16)

    width = HALF // PIECES
    length = (half_ring - 1) * PIECES + PIECES // 2

    def piece_of(direction, k):
        return (k % PIECES + direction * (PIECES // 2)) % PIECES

    def columns(p):
        return pl.ds(p * width, width + (LANES if p == PIECES - 1 else 0))

    def ring_copy(direction, k):
        step = k // PIECES
        source = chip(-step if direction == 0 else step) * n_img + core
        block = gat.at[source, :, columns(piece_of(direction, k))]
        return pltpu.make_async_remote_copy(
            src_ref=block,
            dst_ref=block,
            send_sem=ring_send.at[direction, k],
            recv_sem=ring_recv.at[direction, k],
            device_id={"orient": chip(1 if direction == 0 else -1), "img": core},
            device_id_type=MESH,
        )

    def ring_arrival(direction, k):
        step = 1 + k // PIECES
        source = chip(-step if direction == 0 else step) * n_img + core
        block = gat.at[source, :, columns(piece_of(direction, k))]
        return pltpu.make_async_remote_copy(
            src_ref=block,
            dst_ref=block,
            send_sem=ring_send.at[direction, k],
            recv_sem=ring_recv.at[direction, k],
            device_id={"orient": chip(1 if direction == 0 else -1), "img": core},
            device_id_type=MESH,
        )

    def sib_copy(index, delta, p, side):
        source = chip(delta) * n_img + (core if side == 0 else 1 - core)
        block = gat.at[source, :, columns(p)]
        return pltpu.make_async_remote_copy(
            src_ref=block,
            dst_ref=block,
            send_sem=sib_send.at[index],
            recv_sem=sib_recv.at[index],
            device_id={"orient": orient, "img": 1 - core},
            device_id_type=MESH,
        )

    def sib_args(direction, k):
        step = 1 + k // PIECES
        return (
            PIECES + 2 * k + direction,
            -step if direction == 0 else step,
            piece_of(direction, k),
        )

    pl.semaphore_wait(barrier, n_dev - 1)
    for k in range(PIECES):
        for direction in range(2):
            ring_copy(direction, k).start()
    for p in range(PIECES):
        sib_copy(p, 0, p, 0).start()

    def power_chunks(first, last):
        def step(j, acc):
            start = pl.multiple_of(j * 512, 512)
            re = proj[:, pl.ds(start, 512)].astype(jnp.float32)
            im = proj[:, pl.ds(pl.multiple_of(HALF + start, 512), 512)].astype(jnp.float32)
            parts = split3(re * re + im * im)
            table = ctf[:, pl.ds(start, 512)]
            t_hi, t_mid, t_low = split3(table * table)
            pair = jnp.concatenate(
                [t_hi.astype(jnp.float32), t_mid.astype(jnp.float32), t_low.astype(jnp.float32)], 0
            ).astype(jnp.bfloat16)
            for part in parts:
                acc = acc + dot32(pair, part, NT)
            return acc

        acc = jnp.zeros((3 * ctf.shape[0], n_proj), jnp.float32)
        acc = lax.fori_loop(first, last, step, acc)
        n = ctf.shape[0]
        total = acc[:n] + acc[n : 2 * n] + acc[2 * n :]
        per_group[...] = total if first == 0 else per_group[...] + total

    def prior_row():
        hot = (lax.broadcasted_iota(jnp.int32, (n_ang, n_proj), 0) == angles).astype(jnp.float32)
        hot = hot.astype(jnp.bfloat16)
        total = jnp.zeros((n_cls, n_proj), jnp.float32)
        for part in split3(prior[...]):
            total = total + lax.dot_general(
                part, hot, (((1,), (0,)), ((), ())), preferred_element_type=jnp.float32
            )
        own = lax.broadcasted_iota(jnp.int32, (n_cls, n_proj), 0) == classes
        return jnp.sum(jnp.where(own, total, 0.0), axis=0, keepdims=True)

    def score(blocks, pieces, fresh):
        a = jnp.zeros((len(blocks) * 2 * rows, n_proj), jnp.float32)
        b = a
        for p in pieces:
            left = jnp.concatenate([gat[d, :, p * width : (p + 1) * width] for d in blocks], axis=0)
            a = a + dot32(left, proj[:, p * width : (p + 1) * width], NT)
            b = b + dot32(left, proj[:, HALF + p * width : HALF + (p + 1) * width], NT)
        for i, d in enumerate(blocks):
            base = 2 * rows * i
            part = a[base : base + rows] + b[base + rows : base + 2 * rows]
            scores[d] = part if fresh else scores[d] + part

    def both(delta):
        return [chip(delta) * n_img, chip(delta) * n_img + 1]

    out_copies = []

    def put_out(blocks):
        for d in blocks:
            copy = pltpu.make_async_copy(gat.at[d], g_out.at[d], out_sem.at[len(out_copies)])
            copy.start()
            out_copies.append(copy)

    def await_sib(first, end):
        for q in range(first, end):
            for direction in range(2):
                index, delta, p = sib_args(direction, q)
                sib_copy(index, delta, p, 1).wait_recv()

    early, late = (0, 2), (1, 3)
    last = half_ring - 1
    n_power = HALF // 512
    for k in range(length):
        for direction in range(2):
            ring_arrival(direction, k).wait_recv()
            ahead = k + PIECES
            if ahead < length:
                ring_copy(direction, ahead).start()
            index, delta, p = sib_args(direction, k)
            sib_copy(index, delta, p, 0).start()
        if k == 0:
            for load in loads[4:]:
                load.wait()
            classes = slice_class[...]
            angles = slice_angle[...]
            prior_here = prior_row()
        elif k <= 4:
            power_chunks((k - 1) * n_power // 4, k * n_power // 4)
        step = (k - 1) // PIECES
        if k % PIECES == 1 and 1 <= step < last:
            await_sib(step * PIECES - PIECES, step * PIECES)
            blocks = both(-step) + both(step)
            if step == 1:
                for q in range(PIECES):
                    sib_copy(q, 0, q, 1).wait_recv()
                blocks = both(0) + blocks
            score(blocks, early, True)
            put_out(blocks)
        if k % PIECES == 2 and 1 <= step < last:
            score(blocks, late, False)
        if k == last * PIECES:
            await_sib(k - PIECES, k)
            blocks = both(-last) + both(last)
            score(blocks, early, True)
            put_out(blocks)
    await_sib(last * PIECES, length - 1)
    score(both(half_ring), early, True)
    await_sib(length - 1, length)
    blocks = blocks + both(half_ring)
    put_out(both(half_ring))
    score(blocks, late, False)

    tags = gat[:, :, HALF : HALF + LANES].astype(jnp.float32)
    tags = tags[:, :rows, :].reshape(n_all, LANES)
    tag_col = tags[:, 0:1]
    full = scores[...].reshape(n_all, n_proj)
    energy = jnp.zeros((n_all, n_proj), jnp.float32)
    for h in range(ctf.shape[0]):
        energy = jnp.where(tag_col == h, per_group[h : h + 1, :], energy)
    full = full - 0.5 * energy + prior_here
    top = jnp.max(full, axis=1, keepdims=True)
    expo = jnp.exp(full - top)
    slot = lax.broadcasted_iota(jnp.int32, (LANES, n_proj), 0)
    hot = jnp.where(slot == n_cls, 1.0, jnp.where(slot == classes, 1.0, 0.0)).astype(jnp.bfloat16)
    mass = jnp.zeros((n_all, LANES), jnp.float32)
    for part in split3(expo):
        mass = mass + dot32(part, hot, NT)
    mass = jnp.where(lax.broadcasted_iota(jnp.int32, (n_all, LANES), 1) == n_cls + 1, top, mass)
    turned = mass.T
    stat_src[...] = turned[n_cls : n_cls + 2, :]
    own_src[...] = mass.reshape(n_dev, rows, LANES)

    def stat_copy(r):
        other = (me + r) % n_dev
        return pltpu.make_async_remote_copy(
            src_ref=stat_src,
            dst_ref=stat_dst.at[me],
            send_sem=stat_send.at[r],
            recv_sem=stat_recv.at[r],
            device_id={"orient": other // n_img, "img": other % n_img},
            device_id_type=MESH,
        )

    def own_copy(r):
        other = (me + r) % n_dev
        return pltpu.make_async_remote_copy(
            src_ref=own_src.at[other],
            dst_ref=own_dst.at[me],
            send_sem=own_send.at[r],
            recv_sem=own_recv.at[r],
            device_id={"orient": other // n_img, "img": other % n_img},
            device_id_type=MESH,
        )

    def stat_arrival(r):
        source = (me - r + n_dev) % n_dev
        return pltpu.make_async_remote_copy(
            src_ref=stat_src,
            dst_ref=stat_dst.at[source],
            send_sem=stat_send.at[r],
            recv_sem=stat_recv.at[r],
            device_id={"orient": source // n_img, "img": source % n_img},
            device_id_type=MESH,
        )

    def own_arrival(r):
        source = (me - r + n_dev) % n_dev
        return pltpu.make_async_remote_copy(
            src_ref=own_src.at[source],
            dst_ref=own_dst.at[source],
            send_sem=own_send.at[r],
            recv_sem=own_recv.at[r],
            device_id={"orient": source // n_img, "img": source % n_img},
            device_id_type=MESH,
        )

    for r in range(1, n_dev):
        stat_copy(r).start()
    for r in range(1, n_dev):
        own_copy(r).start()
    stat_dst[me] = stat_src[...]
    own_dst[me] = own_src[me]
    for r in range(1, n_dev):
        stat_arrival(r).wait_recv()
    best = stat_dst[0, 1:2, :]
    for d in range(1, n_dev):
        best = jnp.maximum(best, stat_dst[d, 1:2, :])
    total = jnp.zeros_like(best)
    for d in range(n_dev):
        total = total + jnp.exp(stat_dst[d, 1:2, :] - best) * stat_dst[d, 0:1, :]
    factor = jnp.exp(stat_src[1:2, :] - best) / total
    factor = jnp.broadcast_to(factor, (LANES, n_all)).T[:, 0:1]
    weights = (expo * factor).astype(jnp.bfloat16)
    spread_r = lax.broadcasted_iota(jnp.int32, (n_all, 2 * n_all), 0)
    spread_c = lax.broadcasted_iota(jnp.int32, (n_all, 2 * n_all), 1)
    place = 2 * rows * (spread_r // rows) + spread_r % rows
    for part in range(2):
        spread = jnp.where(spread_c == place + part * rows, 1.0, 0.0).astype(jnp.bfloat16)
        w_out[part] = dot32(weights, spread, TN).astype(jnp.bfloat16)
    lanes = lax.broadcasted_iota(jnp.int32, (n_all, LANES), 1).astype(jnp.float32)
    member = jnp.where(tags == lanes, 1.0, 0.0).astype(jnp.bfloat16)
    mass_out[...] = dot32(member, weights, TN)[: ctf.shape[0]]

    for r in range(1, n_dev):
        own_arrival(r).wait_recv()
    best = own_dst[0, :, n_cls + 1 : n_cls + 2]
    for d in range(1, n_dev):
        best = jnp.maximum(best, own_dst[d, :, n_cls + 1 : n_cls + 2])
    sums = jnp.zeros((rows, LANES), jnp.float32)
    for d in range(n_dev):
        sums = sums + jnp.exp(own_dst[d, :, n_cls + 1 : n_cls + 2] - best) * own_dst[d]
    total = sums[:, n_cls : n_cls + 1]
    cls_out[...] = sums[:, :n_cls] / total
    evidence = best + jnp.log(total)
    lev_out[...] = jnp.sum(jnp.where(diagonal, evidence, 0.0), axis=0, keepdims=True)

    for direction in range(2):
        for k in range(length):
            ring_copy(direction, k).wait_send()
            index, delta, p = sib_args(direction, k)
            sib_copy(index, delta, p, 0).wait_send()
    for p in range(PIECES):
        sib_copy(p, 0, p, 0).wait_send()
    for r in range(1, n_dev):
        stat_copy(r).wait_send()
        own_copy(r).wait_send()
    for copy in out_copies:
        copy.wait()


def sum_kernel(
    g_hbm, w, mass_ref, cls_ref, lev_ref, out, mass_out, cls_out, lev_out, g, held, g_sems, sems
):
    n_proj = out.shape[0]
    weights = w[...].reshape(2 * n_proj, w.shape[2])
    loads = []
    for j in range(HALF // TILE):
        at = pl.ds(j * TILE, TILE)
        loads.append(pltpu.make_async_copy(g_hbm.at[:, :, at], g.at[:, :, at], g_sems.at[j]))
        loads[-1].start()
    copies = []
    for j in range(HALF // TILE):
        loads[j].wait()
        block = g[:, :, j * TILE : (j + 1) * TILE].reshape(w.shape[2], TILE)
        sums = jnp.dot(weights, block, preferred_element_type=jnp.float32).astype(jnp.bfloat16)
        for part in range(2):
            at = pl.ds(part * HALF + j * TILE, TILE)
            held[:, at] = sums[part * n_proj : (part + 1) * n_proj]
            copy = pltpu.make_async_copy(held.at[:, at], out.at[:, at], sems.at[2 * j + part])
            copy.start()
            copies.append(copy)
    mass_out[...] = mass_ref[...]
    cls_out[...] = cls_ref[...]
    lev_out[...] = lev_ref[...]
    for copy in copies:
        copy.wait()


def body(
    n_orient,
    n_img,
    images,
    image_shift,
    image_group,
    projections,
    slice_class,
    slice_angle,
    log_prior,
    ctf_table,
):
    n_dev = n_orient * n_img
    rows = images.shape[0]
    n_all = n_dev * rows
    n_proj, feat = projections.shape
    n_grp = ctf_table.shape[0]
    n_cls = log_prior.shape[0]
    length = (n_orient // 2 - 1) * PIECES + PIECES // 2
    vmem = pl.BlockSpec(memory_space=pltpu.VMEM)
    hbm = pl.BlockSpec(memory_space=pltpu.HBM)
    i32 = jnp.int32
    f32, bf16 = jnp.float32, jnp.bfloat16
    dma = pltpu.SemaphoreType.DMA
    g, w, mass, cls, lev = pl.pallas_call(
        functools.partial(gather_kernel, n_orient, n_img, rows),
        out_shape=(
            jax.ShapeDtypeStruct((n_dev, 2 * rows, HALF + LANES), bf16),
            jax.ShapeDtypeStruct((2, n_proj, 2 * n_all), bf16),
            jax.ShapeDtypeStruct((n_grp, n_proj), f32),
            jax.ShapeDtypeStruct((rows, n_cls), f32),
            jax.ShapeDtypeStruct((1, rows), f32),
        ),
        in_specs=[hbm] * 8,
        out_specs=(hbm, vmem, vmem, vmem, vmem),
        scratch_shapes=[
            pltpu.VMEM(images.shape, bf16),
            pltpu.VMEM((2, rows), i32),
            pltpu.VMEM((1, rows), i32),
            pltpu.VMEM((n_proj, feat), bf16),
            pltpu.VMEM((1, n_proj), i32),
            pltpu.VMEM((1, n_proj), i32),
            pltpu.VMEM(log_prior.shape, f32),
            pltpu.VMEM(ctf_table.shape, f32),
            pltpu.VMEM((n_dev, 2 * rows, HALF + LANES), bf16),
            pltpu.VMEM((n_dev, rows, n_proj), f32),
            pltpu.VMEM((n_grp, n_proj), f32),
            pltpu.VMEM((2, n_all), f32),
            pltpu.VMEM((n_dev, 2, n_all), f32),
            pltpu.VMEM((n_dev, rows, LANES), f32),
            pltpu.VMEM((n_dev, rows, LANES), f32),
            dma((8,)),
            dma((2, length)),
            dma((2, length)),
            dma((2 * length + PIECES,)),
            dma((2 * length + PIECES,)),
            dma((n_dev,)),
            dma((n_dev,)),
            dma((n_dev,)),
            dma((n_dev,)),
            dma((n_dev,)),
        ],
        compiler_params=pltpu.CompilerParams(
            collective_id=0, has_side_effects=True, vmem_limit_bytes=VMEM_BYTES
        ),
    )(
        images,
        image_shift.T,
        image_group.reshape(1, rows),
        projections,
        slice_class.reshape(1, n_proj),
        slice_angle.reshape(1, n_proj),
        log_prior,
        ctf_table,
    )
    out, mass, cls, lev = pl.pallas_call(
        sum_kernel,
        out_shape=(
            jax.ShapeDtypeStruct((n_proj, feat), bf16),
            jax.ShapeDtypeStruct(mass.shape, f32),
            jax.ShapeDtypeStruct(cls.shape, f32),
            jax.ShapeDtypeStruct(lev.shape, f32),
        ),
        in_specs=[hbm, vmem, vmem, vmem, vmem],
        out_specs=(hbm, vmem, vmem, vmem),
        scratch_shapes=[
            pltpu.VMEM((n_dev, 2 * rows, HALF), bf16),
            pltpu.VMEM((n_proj, feat), bf16),
            dma((HALF // TILE,)),
            dma((2 * (HALF // TILE),)),
        ],
        compiler_params=pltpu.CompilerParams(vmem_limit_bytes=VMEM_BYTES),
    )(g, w, mass, cls, lev)
    return out, mass, cls, lev.reshape(rows)


def solution(mesh):
    in_specs = (
        P(("groups", "orient", "img"), None),
        P(("groups", "orient", "img"), None),
        P(("groups", "orient", "img")),
        P(("orient", "img"), None),
        P(("orient", "img")),
        P(("orient", "img")),
        P(),
        P(),
    )
    out_specs = (
        P(("groups", "orient", "img"), None),
        P(None, ("groups", "orient", "img")),
        P(("groups", "orient", "img"), None),
        P(("groups", "orient", "img")),
    )
    return jax.shard_map(
        functools.partial(body, mesh.shape["orient"], mesh.shape["img"]),
        mesh=mesh,
        in_specs=in_specs,
        out_specs=out_specs,
        check_vma=False,
    )
```
